256 devices in a mesh: dp: 32 (over y, z), tensor: 8 (over x, core).
Axes of the slice: x: 4, y: 4, z: 8, core: 2. Of those that a mesh axis runs over, the one named last changes fastest.
Arguments:
- tokens: bfloat16 [8192, 4096], P('dp', 'tensor'), may hold values from -6 to 6
- grad_out: bfloat16 [8192, 12288], P('dp', 'tensor'), may hold values from -0.0625 to 0.0625
- projector: bfloat16 [4096, 512], replicated, may hold values from -0.09375 to 0.09375
- moment_one: float32 [512, 12288], P('dp', 'tensor'), may hold values from -1.75 to 1.75
- moment_two: float32 [512, 12288], P('dp', 'tensor'), may hold values from 0.1 to 2
- weight: bfloat16 [4096, 12288], P('dp', 'tensor'), may hold values from -0.09375 to 0.09375
- next_tokens: bfloat16 [16384, 4096], P('dp', 'tensor'), may hold values from -6 to 6
Outputs:
- gate_out: bfloat16 [16384, 12288], P('dp', 'tensor')
- new_first: float32 [512, 12288], P('dp', 'tensor')
- new_second: float32 [512, 12288], P('dp', 'tensor')
The draws below stay inside these ranges and needn't reach their ends.
All inputs are finite; a program needn't handle non-finite values.
Results may differ from the reference program's by a relative error of at most 0.0045.
The reference program's roundings to bfloat16 on the way (of `reduced`, `normed` and `new_weight`) count: a program that leaves them out, or rounds other values in their place, can miss the bound.
Values may be sent and summed in bfloat16 or wider, within the bound.
No kernel may reach another device: no remote copies, remote signals or barrier semaphores. Data moves between devices by JAX's collectives and lax.ppermute only.
A program may use at most 64 MiB of HBM per device.

```python
import math
import jax
import jax.numpy as jnp
from jax import lax

D = 4096
FF = 12288
RANK = 512
ADAM_STEP = 100
TOKENS = 8192
FWD_TOKENS = 16384


def steps_of(key, shape, pieces, low, top_value):
    loudness, own = 1.0, jax.random.fold_in(key, 6)
    for axis_at, shards_of in pieces:
        draws = jnp.exp(jax.random.uniform(jax.random.fold_in(own, axis_at), (shards_of,), jnp.float32, low / len(pieces), top_value / len(pieces)))
        loudness = loudness * jnp.repeat(draws, shape[axis_at] // shards_of).reshape([-1 if axis == axis_at else 1 for axis in range(len(shape))])
    return loudness


def normal_values(key, shape, deviation, most, cuts=(), kind=jnp.bfloat16):
    result = jax.random.normal(key, shape, jnp.float32) * deviation
    if len(cuts) > 0:
        result = steps_of(key, shape, cuts, -0.22, 0.18) * result
    return jnp.clip(result, min=-most, max=most).astype(kind)


def setup_inputs(seed: int = 0) -> dict:
    arg_keys = jax.random.split(jax.random.key(seed), 8)
    tokens = normal_values(arg_keys[0], (TOKENS, D), 1.0, 6.0, ((0, 32), (1, 8)))
    grad_out = normal_values(arg_keys[1], (TOKENS, FF), (TOKENS ** -0.5), 0.0625, ((0, 32), (1, 8)))
    projector = normal_values(arg_keys[2], (D, RANK), D ** -0.5, 0.09375)
    moment_one = normal_values(arg_keys[3], (RANK, FF), 0.3, 1.75, ((0, 32), (1, 8)), jnp.float32)
    moment_two = jnp.clip(jnp.exp(math.log(2.0) - 2.9957323 * jax.random.uniform(arg_keys[4], (RANK, FF), jnp.float32) ** steps_of(arg_keys[4], (RANK, FF), ((0, 32), (1, 8)), -0.2, 0.2)), 0.1, 2.0)
    weight = normal_values(arg_keys[5], (D, FF), D ** -0.5, 0.09375, ((0, 32), (1, 8)))
    next_tokens = normal_values(arg_keys[6], (FWD_TOKENS, D), 1.0, 6.0, ((0, 32), (1, 8)))
    return {"tokens": tokens, "grad_out": grad_out, "projector": projector, "moment_one": moment_one, "moment_two": moment_two, "weight": weight, "next_tokens": next_tokens}


beta_one = 0.9
beta_two = 0.95
step_size = 0.02
epsilon = 1e-08

def product(left, right):
    return jnp.dot(left.astype(jnp.float32), right.astype(jnp.float32), preferred_element_type=jnp.float32)

def reference(tokens, grad_out, projector, moment_one, moment_two, weight, next_tokens):
    reduced = product(tokens, projector).astype(jnp.bfloat16)
    low_grad = lax.dot_general(reduced.astype(jnp.float32), grad_out.astype(jnp.float32), (((0,), (0,)), ((), ())), preferred_element_type=jnp.float32)
    new_first = beta_one * moment_one + (1.0 - beta_one) * low_grad
    new_second = beta_two * moment_two + (1.0 - beta_two) * low_grad * low_grad
    first_fix = 1.0 - beta_one ** ADAM_STEP
    second_fix = 1.0 - beta_two ** ADAM_STEP
    normed = (new_first / first_fix / (jnp.sqrt(new_second / second_fix) + epsilon)).astype(jnp.bfloat16)
    change = product(projector, normed)
    new_weight = (weight.astype(jnp.float32) - step_size * change).astype(jnp.bfloat16)
    gate_out = product(next_tokens, new_weight).astype(jnp.bfloat16)
    return (gate_out, new_first, new_second)
```

```python
import jax
import jax.numpy as jnp
from jax import lax
from jax.sharding import Mesh, PartitionSpec as P

ADAM_STEP = 100


beta_one = 0.9
beta_two = 0.95
step_size = 0.02
epsilon = 1e-08

SIZES = {"y": 4, "z": 8, "x": 4, "c": 2}
f32, bf16 = jnp.float32, jnp.bfloat16


def shift(block, axis, by):
    size = SIZES[axis]
    return lax.ppermute(block, axis, [(i, (i + by) % size) for i in range(size)])


def gather_x(block):
    half = block.shape[0] // 2
    before = shift(block, "x", 1)
    after = shift(block, "x", -1)
    low = shift(before[:half], "x", 1)
    high = shift(after[half:], "x", -1)
    return [block, before, after, jnp.concatenate([low, high], 0)]


def x_order():
    x = lax.axis_index("x")
    return [x, (x + 3) % 4, (x + 1) % 4, (x + 2) % 4]


def scatter_sum(part, axis):
    size = SIZES[axis]
    me = lax.axis_index(axis)
    total = lax.dynamic_index_in_dim(part, me, 0, keepdims=False).astype(f32)
    arrived = [
        shift(lax.dynamic_index_in_dim(part, (me + by) % size, 0, keepdims=False), axis, by)
        for by in range(1, size)
    ]
    for block in arrived:
        total = total + block.astype(f32)
    return total


def gather_ring(block, axis):
    size = SIZES[axis]
    me = lax.axis_index(axis)
    out = jnp.zeros((size, *block.shape), block.dtype)
    out = lax.dynamic_update_index_in_dim(out, block, me, 0)
    for by in range(1, size):
        out = lax.dynamic_update_index_in_dim(out, shift(block, axis, by), (me - by) % size, 0)
    return out


def body(tokens, grad_out, projector, moment_one, moment_two, weight, next_tokens):
    rows, width = tokens.shape
    core = lax.axis_index("c")

    def proj_of(x, c):
        return lax.dynamic_slice_in_dim(projector, (2 * x + c) * width, width, 0)

    full_weight = lax.all_gather(weight, ("y", "z"), axis=0, tiled=True)

    partial = 0.0
    for x, block in zip(x_order(), gather_x(tokens)):
        partial = partial + jnp.dot(block, proj_of(x, core), preferred_element_type=f32)
    reduced = (partial + shift(partial, "c", 1)).astype(bf16)

    part = lax.dot_general(
        reduced, grad_out, (((0,), (0,)), ((), ())), preferred_element_type=f32
    ).astype(bf16)
    columns = part.shape[1]
    part = part.reshape(4, 8, 16, columns)
    cut = columns // 2
    one = jnp.swapaxes(part[..., :cut], 0, 1)
    one = scatter_sum(scatter_sum(one, "z"), "y")
    two = scatter_sum(scatter_sum(part[..., cut:], "y"), "z")
    low_grad = jnp.concatenate([one, two], 1)

    new_first = beta_one * moment_one + (1.0 - beta_one) * low_grad
    new_second = beta_two * moment_two + (1.0 - beta_two) * low_grad * low_grad
    first_fix = 1.0 - beta_one**ADAM_STEP
    second_fix = 1.0 - beta_two**ADAM_STEP
    normed = (new_first / first_fix / (jnp.sqrt(new_second / second_fix) + epsilon)).astype(bf16)
    one = gather_ring(gather_ring(normed[:, :cut], "z"), "y")
    two = jnp.swapaxes(gather_ring(gather_ring(normed[:, cut:], "y"), "z"), 0, 1)
    full_normed = jnp.concatenate([one, two], 3).reshape(512, columns)

    mine = jnp.concatenate(gather_x(next_tokens), 1)
    other = shift(mine, "c", 1)
    full_next = jnp.zeros((next_tokens.shape[0], 8 * width), bf16)
    for at, x in enumerate(x_order()):
        for held, c in ((mine, core), (other, 1 - core)):
            full_next = lax.dynamic_update_slice_in_dim(
                full_next, held[:, at * width : (at + 1) * width], (2 * x + c) * width, 1
            )
    low_next = jnp.dot(full_next, projector, preferred_element_type=f32).astype(bf16)
    gate = jnp.dot(full_next, full_weight, preferred_element_type=f32)
    gate = gate - step_size * jnp.dot(low_next, full_normed, preferred_element_type=f32)
    return (gate.astype(bf16), new_first, new_second)


def solution(mesh):
    split = Mesh(mesh.devices.reshape(4, 8, 4, 2), ("y", "z", "x", "c"))
    both = P(("y", "z"), ("x", "c"))
    return jax.shard_map(
        body,
        mesh=split,
        in_specs=(both, both, P(), both, both, both, both),
        out_specs=(both, both, both),
        check_vma=False,
    )
```

```python
import functools

import jax
import jax.numpy as jnp
from jax import lax
from jax.experimental import pallas as pl
from jax.experimental.pallas import tpu as pltpu
from jax.sharding import Mesh, PartitionSpec as P

ADAM_STEP = 100


beta_one = 0.9
beta_two = 0.95
step_size = 0.02
epsilon = 1e-08

SIZES = {"y": 4, "z": 8, "x": 4, "c": 2}
f32, bf16 = jnp.float32, jnp.bfloat16


def shift(block, axis, by):
    size = SIZES[axis]
    return lax.ppermute(block, axis, [(i, (i + by) % size) for i in range(size)])


def both_ways(up, down, axis):
    return shift(up, axis, 1), shift(down, axis, -1)


def relay(below, above, axis):
    half = below.shape[0] // 2
    return both_ways(below[:half], above[half:], axis)


def order_four(axis):
    me = lax.axis_index(axis)
    return [me, (me + 3) % 4, (me + 1) % 4, (me + 2) % 4]


def pick(part, at):
    return lax.dynamic_index_in_dim(part, at, 0, keepdims=False)


together = lax.optimization_barrier


def product_kernel(blocks_ref, mine_ref, other_ref, left_ref, right_ref, out_ref):
    step = pl.program_id(0)
    value = jnp.dot(mine_ref[0], left_ref[...], preferred_element_type=f32)
    value += jnp.dot(other_ref[0], right_ref[...], preferred_element_type=f32)

    @pl.when(step == 0)
    def _():
        out_ref[...] = value

    @pl.when(step > 0)
    def _():
        out_ref[...] += value


def product(mine, other, right, blocks):
    steps, rows, depth = mine.shape
    columns = right.shape[1]
    return pl.pallas_call(
        product_kernel,
        out_shape=jax.ShapeDtypeStruct((rows, columns), f32),
        grid_spec=pltpu.PrefetchScalarGridSpec(
            num_scalar_prefetch=1,
            grid=(steps,),
            in_specs=[
                pl.BlockSpec((1, rows, depth), lambda i, blocks: (i, 0, 0)),
                pl.BlockSpec((1, rows, depth), lambda i, blocks: (i, 0, 0)),
                pl.BlockSpec((depth, columns), lambda i, blocks: (blocks[i], 0)),
                pl.BlockSpec((depth, columns), lambda i, blocks: (blocks[steps + i], 0)),
            ],
            out_specs=pl.BlockSpec((rows, columns), lambda i, blocks: (0, 0)),
        ),
        compiler_params=pltpu.CompilerParams(vmem_limit_bytes=32 << 20),
        cost_estimate=pl.CostEstimate(
            flops=4 * steps * rows * depth * columns,
            bytes_accessed=4 * steps * depth * (rows + columns) + 4 * rows * columns,
            transcendentals=0,
        ),
    )(blocks, mine, other, right, right)


def last_kernel(blocks_ref, mine_ref, other_ref, weight_ref, low_ref, normed_ref, out_ref):
    steps, _, depth = mine_ref.shape
    value = -step_size * jnp.dot(low_ref[...], normed_ref[...], preferred_element_type=f32)
    for i in range(steps):
        for held, at in ((mine_ref, i), (other_ref, steps + i)):
            start = pl.multiple_of(blocks_ref[at] * depth, depth)
            value += jnp.dot(
                held[i], weight_ref[pl.ds(start, depth), :], preferred_element_type=f32
            )
    out_ref[...] = value.astype(bf16)


def last(mine, other, weight, low, normed, blocks):
    steps, rows, depth = mine.shape
    features, columns = weight.shape
    rank, tile = low.shape[1], 256

    def whole(array):
        return pl.BlockSpec(array.shape, lambda j, blocks: (0,) * array.ndim)

    return pl.pallas_call(
        last_kernel,
        out_shape=jax.ShapeDtypeStruct((rows, columns), bf16),
        grid_spec=pltpu.PrefetchScalarGridSpec(
            num_scalar_prefetch=1,
            grid=(columns // tile,),
            in_specs=[
                whole(mine),
                whole(other),
                pl.BlockSpec((features, tile), lambda j, blocks: (0, j)),
                whole(low),
                pl.BlockSpec((rank, tile), lambda j, blocks: (0, j)),
            ],
            out_specs=pl.BlockSpec((rows, tile), lambda j, blocks: (0, j)),
        ),
        compiler_params=pltpu.CompilerParams(vmem_limit_bytes=52 << 20),
        cost_estimate=pl.CostEstimate(
            flops=2 * rows * (features + rank) * columns,
            bytes_accessed=2 * (features * (rows + columns) + rank * columns + rows * columns),
            transcendentals=0,
        ),
    )(blocks, mine, other, weight, low, normed)


def body(tokens, grad_out, projector, moment_one, moment_two, weight, next_tokens):
    rows, width = tokens.shape
    columns = weight.shape[1]
    core = lax.axis_index("c")
    x_places, y_places = order_four("x"), order_four("y")

    def proj_of(x, c):
        return lax.dynamic_slice_in_dim(projector, (2 * x + c) * width, width, 0)

    def part_of(x, block):
        return jnp.dot(block, proj_of(x, core), preferred_element_type=f32)

    gathered = lax.all_gather(weight, ("y", "z"), axis=0, tiled=True)

    below, above = both_ways(tokens, tokens, "x")
    partial = part_of(x_places[0], tokens)
    below, above, partial = together((below, above, partial))

    low, high = relay(below, above, "x")
    partial = partial + part_of(x_places[1], below) + part_of(x_places[2], above)
    low, high, partial = together((low, high, partial))

    partial = partial + part_of(x_places[3], jnp.concatenate([low, high], 0))
    reduced = (partial + shift(partial, "c", 1)).astype(bf16)
    part = lax.dot_general(
        reduced, grad_out, (((0,), (0,)), ((), ())), preferred_element_type=f32
    ).astype(bf16)
    part, next_tokens = together((part, next_tokens))

    part = part.reshape(4, -1, columns)
    half = part.shape[1] // 2
    distant = pick(part, y_places[3])
    low, high = both_ways(distant[:half], distant[half:], "y")
    low, high, next_tokens = together((low, high, next_tokens))

    up, down = pick(part, y_places[2]).astype(f32), pick(part, y_places[1]).astype(f32)
    up = jnp.concatenate([up[:half] + low.astype(f32), up[half:]], 0).astype(bf16)
    down = jnp.concatenate([down[:half], down[half:] + high.astype(f32)], 0).astype(bf16)
    below, above = both_ways(up, down, "y")
    next_below, next_above = both_ways(next_tokens, next_tokens, "x")
    summed = pick(part, y_places[0]).astype(f32) + below.astype(f32) + above.astype(f32)
    summed = summed.astype(bf16).reshape(8, -1, columns)
    summed, next_below, next_above = together((summed, next_below, next_above))

    low_grad = lax.all_to_all(summed, "z", 0, 0)
    next_far = jnp.concatenate(relay(next_below, next_above, "x"), 0)
    low_grad, next_far = together((low_grad, next_far))

    low_grad = jnp.sum(low_grad.astype(f32), 0)
    new_first = beta_one * moment_one + (1.0 - beta_one) * low_grad
    new_second = beta_two * moment_two + (1.0 - beta_two) * low_grad * low_grad
    first_fix = 1.0 - beta_one**ADAM_STEP
    second_fix = 1.0 - beta_two**ADAM_STEP
    normed = (new_first / first_fix / (jnp.sqrt(new_second / second_fix) + epsilon)).astype(bf16)
    normed = lax.all_to_all(jnp.broadcast_to(normed[None], (8, *normed.shape)), "z", 0, 0)
    normed = normed.reshape(-1, columns)
    mine = jnp.stack([next_tokens, next_below, next_above, next_far], 0)
    other = shift(mine, "c", 1)
    normed, other = together((normed, other))

    normed_y = both_ways(normed, normed, "y")
    natural = jnp.stack([2 * x + c for c in (core, 1 - core) for x in x_places])
    low_next = product(mine, other, projector, natural).astype(bf16)
    size = low_next.shape[1] // 4
    low_next = jnp.concatenate(
        [lax.dynamic_slice_in_dim(low_next, y * size, size, 1) for y in y_places], 1
    )
    normed_y, low_next = together((normed_y, low_next))

    normed_far = relay(*normed_y, "y")
    full_normed = jnp.concatenate([normed, *normed_y, *normed_far], 0)
    gate = last(mine, other, gathered, low_next, full_normed, natural)
    return (gate, new_first, new_second)


def solution(mesh):
    split = Mesh(mesh.devices.reshape(4, 8, 4, 2), ("y", "z", "x", "c"))
    both = P(("y", "z"), ("x", "c"))
    return jax.shard_map(
        body,
        mesh=split,
        in_specs=(both, both, P(), both, both, both, both),
        out_specs=(both, both, both),
        check_vma=False,
    )
```

```python
import functools

import jax
import jax.numpy as jnp
from jax import lax
from jax.experimental import pallas as pl
from jax.experimental.pallas import tpu as pltpu
from jax.sharding import Mesh, PartitionSpec as P

ADAM_STEP = 100


beta_one = 0.9
beta_two = 0.95
step_size = 0.02
epsilon = 1e-08

Y = ("yh", "yl")
SIZES = {Y: 4, "z": 8, "x": 4, "c": 2}
f32, bf16 = jnp.float32, jnp.bfloat16


def shift(block, axis, by):
    size = SIZES[axis]
    return lax.ppermute(block, axis, [(i, (i + by) % size) for i in range(size)])


def both_ways(up, down, axis):
    return shift(up, axis, 1), shift(down, axis, -1)


def relay(below, above, axis):
    half = below.shape[0] // 2
    return both_ways(below[:half], above[half:], axis)


def order_four(axis):
    me = lax.axis_index(axis)
    return [me, (me + 3) % 4, (me + 1) % 4, (me + 2) % 4]


def facing(block):
    return lax.ppermute(block, Y, [(i, 3 - i) for i in range(4)])


def beside(block):
    return lax.ppermute(block, Y, [(i, i ^ 1) for i in range(4)])


def pick(part, at):
    return lax.dynamic_index_in_dim(part, at, 0, keepdims=False)


together = lax.optimization_barrier


def prepare_kernel(blocks_ref, places_ref, *refs):
    pieces, (projector_ref, whole_ref, low_ref, sum_ref) = refs[:-4], refs[-4:]
    step = pl.program_id(0)
    depth = pieces[0].shape[1]
    lanes = 128
    count = depth // lanes

    def put(piece, at):
        for i in range(count):
            start = pl.multiple_of(places_ref[at * count + i] * lanes, lanes)
            whole_ref[:, pl.ds(start, lanes)] = piece[:, i * lanes : (i + 1) * lanes]

    def add(piece, at):
        start = pl.multiple_of(blocks_ref[at] * depth, depth)
        return jnp.dot(
            piece[...], projector_ref[pl.ds(start, depth), :], preferred_element_type=f32
        )

    for side, (own, below, above, low, high) in enumerate((pieces[:5], pieces[5:])):
        for i, piece in enumerate((own, below, above)):
            put(piece, 4 * side + i)
        pl.when(step == 0)(functools.partial(put, low, 4 * side + 3))
        pl.when(step == 1)(functools.partial(put, high, 4 * side + 3))

    @pl.when(step == 0)
    def _():
        sum_ref[...] = add(pieces[0], 0)
        for at, piece in ((1, 1), (2, 2), (3, 3), (4, 5), (5, 6), (6, 7)):
            sum_ref[...] += add(pieces[piece], at)
        low_ref[...] = (sum_ref[...] + add(pieces[8], 7)).astype(bf16)


def prepare(mine, other, projector, blocks, places):
    rows, depth = mine[0].shape[0] // 2, mine[0].shape[1]
    features, rank = projector.shape
    moving = pl.BlockSpec((rows, depth), lambda i, *_: (i, 0))
    fixed = pl.BlockSpec((rows, depth), lambda i, *_: (0, 0))
    return pl.pallas_call(
        prepare_kernel,
        out_shape=(
            jax.ShapeDtypeStruct((2 * rows, features), bf16),
            jax.ShapeDtypeStruct((rows, rank), bf16),
        ),
        grid_spec=pltpu.PrefetchScalarGridSpec(
            num_scalar_prefetch=2,
            grid=(2,),
            in_specs=[moving, moving, moving, fixed, fixed] * 2
            + [pl.BlockSpec((features, rank), lambda i, *_: (0, 0))],
            out_specs=(
                pl.BlockSpec((rows, features), lambda i, *_: (i, 0)),
                pl.BlockSpec((rows, rank), lambda i, *_: (0, 0)),
            ),
            scratch_shapes=[pltpu.VMEM((rows, rank), f32)],
        ),
        compiler_params=pltpu.CompilerParams(vmem_limit_bytes=48 << 20),
        cost_estimate=pl.CostEstimate(
            flops=2 * rows * features * rank,
            bytes_accessed=2 * features * (4 * rows + rank),
            transcendentals=0,
        ),
    )(blocks, places, *mine, *other, projector)


def product_kernel(left_ref, right_ref, out_ref):
    value = jnp.dot(left_ref[...], right_ref[...], preferred_element_type=f32)
    out_ref[...] = value.astype(out_ref.dtype)


def product(left, part, rows, right, dtype):
    features, columns = right.shape
    tile = 256
    return pl.pallas_call(
        product_kernel,
        out_shape=jax.ShapeDtypeStruct((rows, columns), dtype),
        grid=(columns // tile,),
        in_specs=[
            pl.BlockSpec((rows, features), lambda j: (part, 0)),
            pl.BlockSpec((features, tile), lambda j: (0, j)),
        ],
        out_specs=pl.BlockSpec((rows, tile), lambda j: (0, j)),
        compiler_params=pltpu.CompilerParams(vmem_limit_bytes=48 << 20),
        cost_estimate=pl.CostEstimate(
            flops=2 * rows * features * columns,
            bytes_accessed=2 * features * (rows + columns) + 4 * rows * columns,
            transcendentals=0,
        ),
    )(left, right)


def last_kernel(group_ref, own_ref, sent_ref, low_ref, *refs):
    normed, out_ref = jnp.concatenate([ref[...] for ref in refs[:-1]], 0), refs[-1]
    step = pl.program_id(0)
    change = -step_size * jnp.dot(low_ref[...], normed, preferred_element_type=f32)

    @pl.when(step == 0)
    def _():
        out_ref[...] = (own_ref[...] + change).astype(bf16)

    @pl.when(step == 1)
    def _():
        out_ref[...] = (sent_ref[...].astype(f32) + change).astype(bf16)


def last(own, sent, low, normed, group):
    rows, columns = own.shape
    rank = low.shape[1]
    place = lambda j, group: (0, (j + group[0]) % 2)
    fixed = lambda j, group: (0, 0)
    return pl.pallas_call(
        last_kernel,
        out_shape=jax.ShapeDtypeStruct((rows, 2 * columns), bf16),
        grid_spec=pltpu.PrefetchScalarGridSpec(
            num_scalar_prefetch=1,
            grid=(2,),
            in_specs=[
                pl.BlockSpec((rows, columns), fixed),
                pl.BlockSpec((rows, columns), fixed),
                pl.BlockSpec((rows, rank), fixed),
                *[pl.BlockSpec((piece.shape[0], columns), place) for piece in normed],
            ],
            out_specs=pl.BlockSpec((rows, columns), place),
        ),
        compiler_params=pltpu.CompilerParams(vmem_limit_bytes=32 << 20),
        cost_estimate=pl.CostEstimate(
            flops=4 * rows * rank * columns,
            bytes_accessed=10 * rows * columns + 4 * rank * columns,
            transcendentals=0,
        ),
    )(group.reshape(1), own, sent, low, *normed)


def body(tokens, grad_out, projector, moment_one, moment_two, weight, next_tokens):
    width = tokens.shape[1]
    columns = weight.shape[1]
    core = lax.axis_index("c")
    x_places, y_places = order_four("x"), order_four(Y)

    def proj_of(x, c):
        return lax.dynamic_slice_in_dim(projector, (2 * x + c) * width, width, 0)

    def part_of(x, block):
        return jnp.dot(block, proj_of(x, core), preferred_element_type=f32)

    y = lax.axis_index(Y)
    side, group = columns // 2, y // 2
    weight_own = lax.dynamic_slice_in_dim(weight, group * side, side, 1)
    weight_facing = facing(lax.dynamic_slice_in_dim(weight, (1 - group) * side, side, 1))
    below, above = both_ways(tokens, tokens, "x")
    partial = part_of(x_places[0], tokens)
    rows = next_tokens.shape[0]
    below, above, partial, weight_facing = together((below, above, partial, weight_facing))

    weight_pair = jnp.concatenate([weight_own, weight_facing], 0)
    weight_beside = beside(weight_pair)
    low, high = relay(below, above, "x")
    facing_next = facing(next_tokens)
    partial = partial + part_of(x_places[1], below) + part_of(x_places[2], above)
    low, high, partial, facing_next, weight_beside = together(
        (low, high, partial, facing_next, weight_beside)
    )

    gathered = lax.all_gather(
        jnp.concatenate([weight_pair, weight_beside], 0), "z", axis=0, tiled=True
    )
    partial = partial + part_of(x_places[3], jnp.concatenate([low, high], 0))
    reduced = (partial + shift(partial, "c", 1)).astype(bf16)
    part = lax.dot_general(
        reduced, grad_out, (((0,), (0,)), ((), ())), preferred_element_type=f32
    ).astype(bf16)
    pair_next = jnp.concatenate([next_tokens, facing_next], 0)
    (part,) = together((part,))

    part = part.reshape(4, -1, columns)
    half = part.shape[1] // 2
    distant = pick(part, y_places[3])
    low, high = both_ways(distant[:half], distant[half:], Y)
    next_below, next_above = both_ways(pair_next, pair_next, "x")
    low, high = together((low, high))

    up, down = pick(part, y_places[2]).astype(f32), pick(part, y_places[1]).astype(f32)
    up = jnp.concatenate([up[:half] + low.astype(f32), up[half:]], 0).astype(bf16)
    down = jnp.concatenate([down[:half], down[half:] + high.astype(f32)], 0).astype(bf16)
    below, above = both_ways(up, down, Y)
    summed = pick(part, y_places[0]).astype(f32) + below.astype(f32) + above.astype(f32)
    (summed,) = together((summed.astype(bf16).reshape(8, -1, columns),))

    low_grad = lax.all_to_all(summed, "z", 0, 0)
    next_low, next_high = relay(next_below, next_above, "x")
    low_grad, next_low, next_high = together((low_grad, next_low, next_high))

    low_grad = jnp.sum(low_grad.astype(f32), 0)
    new_first = beta_one * moment_one + (1.0 - beta_one) * low_grad
    new_second = beta_two * moment_two + (1.0 - beta_two) * low_grad * low_grad
    first_fix = 1.0 - beta_one**ADAM_STEP
    second_fix = 1.0 - beta_two**ADAM_STEP
    normed = (new_first / first_fix / (jnp.sqrt(new_second / second_fix) + epsilon)).astype(bf16)
    normed = lax.all_to_all(jnp.broadcast_to(normed[None], (8, *normed.shape)), "z", 0, 0)
    normed = normed.reshape(-1, columns)
    mine = [pair_next, next_below, next_above, next_low, next_high]
    other = [shift(piece, "c", 1) for piece in mine]
    blocks = [(x, c) for c in (core, 1 - core) for x in x_places]
    natural = jnp.stack([2 * x + c for x, c in blocks])
    gathered_at = []
    for x, c in blocks:
        place = jnp.where(x == y, 0, jnp.where(x == 3 - y, 1, jnp.where(x == y ^ 1, 2, 3)))
        gathered_at += [4 * (4 * c + i) + place for i in range(4)]
    full_next, low_next = prepare(mine, other, projector, natural, jnp.stack(gathered_at))
    size = low_next.shape[1] // 4
    low_next = jnp.concatenate(
        [lax.dynamic_slice_in_dim(low_next, place * size, size, 1) for place in (y, y ^ 1, 3 - y, 3 - (y ^ 1))],
        1,
    )
    normed, full_next, low_next = together((normed, full_next, low_next))

    normed_beside, normed_facing = beside(normed), facing(normed)
    sent = product(full_next, 1, rows, gathered, bf16)
    normed_beside, normed_facing, sent, full_next = together(
        (normed_beside, normed_facing, sent, full_next)
    )

    sent = facing(sent)
    normed_far = beside(normed_facing)
    own = product(full_next, 0, rows, gathered, f32)
    pieces = (normed, normed_beside, normed_facing, normed_far)
    gate = last(own, sent, low_next, pieces, group)
    return (gate, new_first, new_second)


def solution(mesh):
    split = Mesh(mesh.devices.reshape(2, 2, 8, 4, 2), (*Y, "z", "x", "c"))
    both = P((*Y, "z"), ("x", "c"))
    return jax.shard_map(
        body,
        mesh=split,
        in_specs=(both, both, P(), both, both, both, both),
        out_specs=(both, both, both),
        check_vma=False,
    )
```

```python
import functools

import jax
import jax.numpy as jnp
from jax import lax
from jax.experimental import pallas as pl
from jax.experimental.pallas import tpu as pltpu
from jax.sharding import Mesh, PartitionSpec as P

ADAM_STEP = 100


beta_one = 0.9
beta_two = 0.95
step_size = 0.02
epsilon = 1e-08

Y = ("yh", "yl")
SIZES = {Y: 4, "z": 8, "x": 4, "c": 2}
f32, bf16 = jnp.float32, jnp.bfloat16


def shift(block, axis, by):
    size = SIZES[axis]
    return lax.ppermute(block, axis, [(i, (i + by) % size) for i in range(size)])


def both_ways(up, down, axis):
    return shift(up, axis, 1), shift(down, axis, -1)


def relay(below, above, axis):
    half = below.shape[0] // 2
    return both_ways(below[:half], above[half:], axis)


def order_four(axis):
    me = lax.axis_index(axis)
    return [me, (me + 3) % 4, (me + 1) % 4, (me + 2) % 4]


def facing(block):
    return lax.ppermute(block, Y, [(i, 3 - i) for i in range(4)])


def beside(block):
    return lax.ppermute(block, Y, [(i, i ^ 1) for i in range(4)])


def pick(part, at):
    return lax.dynamic_index_in_dim(part, at, 0, keepdims=False)


together = lax.optimization_barrier


def prepare_kernel(blocks_ref, places_ref, *refs):
    pieces, (projector_ref, whole_ref, low_ref, sum_ref) = refs[:-4], refs[-4:]
    step = pl.program_id(0)
    depth = pieces[0].shape[1]
    lanes = 128
    count = depth // lanes

    def put(piece, at):
        for i in range(count):
            start = pl.multiple_of(places_ref[at * count + i] * lanes, lanes)
            whole_ref[:, pl.ds(start, lanes)] = piece[:, i * lanes : (i + 1) * lanes]

    def add(piece, at):
        start = pl.multiple_of(blocks_ref[at] * depth, depth)
        return jnp.dot(
            piece[...], projector_ref[pl.ds(start, depth), :], preferred_element_type=f32
        )

    for side, (own, below, above, low, high) in enumerate((pieces[:5], pieces[5:])):
        for i, piece in enumerate((own, below, above)):
            put(piece, 4 * side + i)
        pl.when(step == 0)(functools.partial(put, low, 4 * side + 3))
        pl.when(step == 1)(functools.partial(put, high, 4 * side + 3))

    @pl.when(step == 0)
    def _():
        sum_ref[...] = add(pieces[0], 0)
        for at, piece in ((1, 1), (2, 2), (3, 3), (4, 5), (5, 6), (6, 7)):
            sum_ref[...] += add(pieces[piece], at)
        low_ref[...] = (sum_ref[...] + add(pieces[8], 7)).astype(bf16)


def prepare(mine, other, projector, blocks, places):
    rows, depth = mine[0].shape[0] // 2, mine[0].shape[1]
    features, rank = projector.shape
    moving = pl.BlockSpec((rows, depth), lambda i, *_: (i, 0))
    fixed = pl.BlockSpec((rows, depth), lambda i, *_: (0, 0))
    return pl.pallas_call(
        prepare_kernel,
        out_shape=(
            jax.ShapeDtypeStruct((2 * rows, features), bf16),
            jax.ShapeDtypeStruct((rows, rank), bf16),
        ),
        grid_spec=pltpu.PrefetchScalarGridSpec(
            num_scalar_prefetch=2,
            grid=(2,),
            in_specs=[moving, moving, moving, fixed, fixed] * 2
            + [pl.BlockSpec((features, rank), lambda i, *_: (0, 0))],
            out_specs=(
                pl.BlockSpec((rows, features), lambda i, *_: (i, 0)),
                pl.BlockSpec((rows, rank), lambda i, *_: (0, 0)),
            ),
            scratch_shapes=[pltpu.VMEM((rows, rank), f32)],
        ),
        compiler_params=pltpu.CompilerParams(vmem_limit_bytes=48 << 20),
        cost_estimate=pl.CostEstimate(
            flops=2 * rows * features * rank,
            bytes_accessed=2 * features * (4 * rows + rank),
            transcendentals=0,
        ),
    )(blocks, places, *mine, *other, projector)


def product_kernel(part_ref, left_ref, one, two, three, four, out_ref, whole_ref):
    half, lanes = one.shape[-2:]
    for i, (first, second) in enumerate(((one, two), (three, four))):
        columns = pl.ds(i * lanes, lanes)
        whole_ref[:, :half, columns] = first[...].reshape(-1, half, lanes)
        whole_ref[:, half:, columns] = second[...].reshape(-1, half, lanes)
    whole = whole_ref[...].reshape(-1, 2 * lanes)
    out_ref[...] = jnp.dot(left_ref[...], whole, preferred_element_type=f32).astype(out_ref.dtype)


def product(left, part, weight, first, tiles, dtype, beside=None):
    rows, features = left.shape[0] // 2, left.shape[1]
    places, blocks, half, lanes = weight.shape
    pairs = blocks // 2 + 1

    def block(at):
        return pl.BlockSpec((places, 1, half, lanes), lambda j, part: (0, at + 2 * j, 0, 0))

    specs = [block(first), block(first + pairs), block(first + 1), block(first + 1 + pairs)]
    arrays = [weight] * 4
    if beside is not None:
        specs[3] = pl.BlockSpec(beside.shape, lambda j, part: (0, 0, 0))
        arrays[3] = beside
    columns = tiles * 2 * lanes
    return pl.pallas_call(
        product_kernel,
        out_shape=jax.ShapeDtypeStruct((rows, columns), dtype),
        grid_spec=pltpu.PrefetchScalarGridSpec(
            num_scalar_prefetch=1,
            grid=(tiles,),
            in_specs=[pl.BlockSpec((rows, features), lambda j, part: (part[0], 0)), *specs],
            out_specs=pl.BlockSpec((rows, 2 * lanes), lambda j, part: (0, j)),
            scratch_shapes=[pltpu.VMEM((places, 2 * half, 2 * lanes), bf16)],
        ),
        compiler_params=pltpu.CompilerParams(vmem_limit_bytes=48 << 20),
        cost_estimate=pl.CostEstimate(
            flops=2 * rows * features * columns,
            bytes_accessed=2 * features * (rows + columns) + 4 * rows * columns,
            transcendentals=0,
        ),
    )(part, left, *arrays)


def changed(value, low_ref, pieces, columns):
    normed = jnp.concatenate([piece[:, columns] for piece in pieces], 0)
    change = jnp.dot(low_ref[...], normed, preferred_element_type=f32)
    return (value.astype(f32) - step_size * change).astype(bf16)


def most_kernel(group_ref, own_one, own_two, sent_one, low_ref, *refs):
    pieces, out_ref = refs[:-1], refs[-1]
    cut = own_one.shape[1]
    first, second = slice(0, cut), slice(cut, out_ref.shape[1])

    @pl.when(pl.program_id(0) == 0)
    def _():
        out_ref[:, first] = changed(own_one[...], low_ref, pieces, first)
        out_ref[:, second] = changed(own_two[...], low_ref, pieces, second)

    @pl.when(pl.program_id(0) == 1)
    def _():
        out_ref[:, first] = changed(sent_one[...], low_ref, pieces, first)


def rest_kernel(group_ref, sent_ref, low_ref, *refs):
    pieces, out_ref = refs[:-2], refs[-1]
    out_ref[...] = changed(sent_ref[...], low_ref, pieces, slice(None))


def last(own, sent, low, normed, group):
    rows, rank = low.shape
    cut, rest = own[0].shape[1], own[1].shape[1]
    columns = cut + rest
    place = lambda j, group: (0, (j + group[0]) % 2)
    fixed = lambda j, group: (0, 0)
    group = group.reshape(1)

    def call(kernel, grid, in_specs, out_spec, width, aliases, *arrays):
        return pl.pallas_call(
            kernel,
            out_shape=jax.ShapeDtypeStruct((rows, 2 * columns), bf16),
            grid_spec=pltpu.PrefetchScalarGridSpec(
                num_scalar_prefetch=1, grid=grid, in_specs=in_specs, out_specs=out_spec
            ),
            input_output_aliases=aliases,
            compiler_params=pltpu.CompilerParams(vmem_limit_bytes=32 << 20),
            cost_estimate=pl.CostEstimate(
                flops=2 * rows * rank * width,
                bytes_accessed=5 * rows * width + 2 * rank * width,
                transcendentals=0,
            ),
        )(group, *arrays)

    most = call(
        most_kernel,
        (2,),
        [
            *[pl.BlockSpec(array.shape, fixed) for array in (*own, sent[0], low)],
            *[pl.BlockSpec((piece.shape[0], columns), place) for piece in normed],
        ],
        pl.BlockSpec((rows, columns), place),
        columns + cut,
        {},
        *own,
        sent[0],
        low,
        *normed,
    )
    at = lambda j, group: (0, (1 - group[0]) * (columns // rest) + cut // rest)
    return call(
        rest_kernel,
        (1,),
        [
            pl.BlockSpec(sent[1].shape, fixed),
            pl.BlockSpec(low.shape, fixed),
            *[pl.BlockSpec((piece.shape[0], rest), at) for piece in normed],
            pl.BlockSpec(memory_space=pl.ANY),
        ],
        pl.BlockSpec((rows, rest), at),
        rest,
        {3 + len(normed): 0},
        sent[1],
        low,
        *normed,
        most,
    )


def body(tokens, grad_out, projector, moment_one, moment_two, weight, next_tokens):
    width = tokens.shape[1]
    columns = weight.shape[1]
    core = lax.axis_index("c")
    x_places, y_places = order_four("x"), order_four(Y)

    def proj_of(x, c):
        return lax.dynamic_slice_in_dim(projector, (2 * x + c) * width, width, 0)

    def part_of(x, block):
        return jnp.dot(block, proj_of(x, core), preferred_element_type=f32)

    y = lax.axis_index(Y)
    side, group = columns // 2, y // 2
    lanes = 128
    count = side // lanes
    blocks = jnp.swapaxes(weight.reshape(-1, 2 * count, lanes), 0, 1)
    weight_own = lax.dynamic_slice_in_dim(blocks, group * count, count, 0)
    weight_facing = facing(lax.dynamic_slice_in_dim(blocks, (1 - group) * count, count, 0))
    below, above = both_ways(tokens, tokens, "x")
    partial = part_of(x_places[0], tokens)
    below, above, partial, weight_facing = together((below, above, partial, weight_facing))

    weight_pair = jnp.concatenate([weight_own, weight_facing], 1)
    weight_beside = beside(weight_pair[:-1])
    low, high = relay(below, above, "x")
    facing_next = facing(next_tokens)
    partial = partial + part_of(x_places[1], below) + part_of(x_places[2], above)
    low, high, partial, facing_next, weight_beside = together(
        (low, high, partial, facing_next, weight_beside)
    )

    gathered = lax.all_gather(jnp.concatenate([weight_pair, weight_beside], 0), "z", axis=0)
    partial = partial + part_of(x_places[3], jnp.concatenate([low, high], 0))
    reduced = (partial + shift(partial, "c", 1)).astype(bf16)
    part = lax.dot_general(
        reduced, grad_out, (((0,), (0,)), ((), ())), preferred_element_type=f32
    ).astype(bf16)
    pair_next = jnp.concatenate([next_tokens, facing_next], 0)
    (part,) = together((part,))

    part = part.reshape(4, -1, columns)
    half = part.shape[1] // 2
    distant = pick(part, y_places[3])
    low, high = both_ways(distant[:half], distant[half:], Y)
    next_below, next_above = both_ways(pair_next, pair_next, "x")
    low, high = together((low, high))

    up, down = pick(part, y_places[2]).astype(f32), pick(part, y_places[1]).astype(f32)
    up = jnp.concatenate([up[:half] + low.astype(f32), up[half:]], 0).astype(bf16)
    down = jnp.concatenate([down[:half], down[half:] + high.astype(f32)], 0).astype(bf16)
    below, above = both_ways(up, down, Y)
    summed = pick(part, y_places[0]).astype(f32) + below.astype(f32) + above.astype(f32)
    (summed,) = together((summed.astype(bf16).reshape(8, -1, columns),))

    low_grad = lax.all_to_all(summed, "z", 0, 0)
    next_low, next_high = relay(next_below, next_above, "x")
    low_grad, next_low, next_high = together((low_grad, next_low, next_high))

    low_grad = jnp.sum(low_grad.astype(f32), 0)
    new_first = beta_one * moment_one + (1.0 - beta_one) * low_grad
    new_second = beta_two * moment_two + (1.0 - beta_two) * low_grad * low_grad
    first_fix = 1.0 - beta_one**ADAM_STEP
    second_fix = 1.0 - beta_two**ADAM_STEP
    normed = (new_first / first_fix / (jnp.sqrt(new_second / second_fix) + epsilon)).astype(bf16)
    normed = lax.all_to_all(jnp.broadcast_to(normed[None], (8, *normed.shape)), "z", 0, 0)
    normed = normed.reshape(-1, columns)
    mine = [pair_next, next_below, next_above, next_low, next_high]
    other = [shift(piece, "c", 1) for piece in mine]
    blocks = [(x, c) for c in (core, 1 - core) for x in x_places]
    natural = jnp.stack([2 * x + c for x, c in blocks])
    gathered_at = []
    for x, c in blocks:
        place = jnp.where(x == y, 0, jnp.where(x == 3 - y, 1, jnp.where(x == y ^ 1, 2, 3)))
        gathered_at += [4 * (4 * c + i) + place for i in range(4)]
    full_next, low_next = prepare(mine, other, projector, natural, jnp.stack(gathered_at))
    size = low_next.shape[1] // 4
    low_next = jnp.concatenate(
        [lax.dynamic_slice_in_dim(low_next, place * size, size, 1) for place in (y, y ^ 1, 3 - y, 3 - (y ^ 1))],
        1,
    )
    normed, full_next, low_next = together((normed, full_next, low_next))

    normed_beside, normed_facing = beside(normed), facing(normed)
    own_part, sent_part = jnp.zeros(1, jnp.int32), jnp.ones(1, jnp.int32)
    late = beside(gathered[:, count - 1])
    tiles = count // 2 - 1
    sent_one = product(full_next, sent_part, gathered, 0, tiles, bf16)
    normed_beside, normed_facing, sent_one, full_next = together(
        (normed_beside, normed_facing, sent_one, full_next)
    )

    sent_one = facing(sent_one)
    normed_far = beside(normed_facing)
    own_one = product(full_next, own_part, gathered, 0, tiles, f32)
    late, own_one, full_next = together((late, own_one, full_next))

    sent_two = product(full_next, sent_part, gathered, count - 2, 1, bf16, late)
    sent_two, full_next = together((sent_two, full_next))

    sent_two = facing(sent_two)
    own_two = product(full_next, own_part, gathered, count - 2, 1, f32, late)
    pieces = (normed, normed_beside, normed_facing, normed_far)
    gate = last((own_one, own_two), (sent_one, sent_two), low_next, pieces, group)
    return (gate, new_first, new_second)


def solution(mesh):
    split = Mesh(mesh.devices.reshape(2, 2, 8, 4, 2), (*Y, "z", "x", "c"))
    both = P((*Y, "z"), ("x", "c"))
    return jax.shard_map(
        body,
        mesh=split,
        in_specs=(both, both, P(), both, both, both, both),
        out_specs=(both, both, both),
        check_vma=False,
    )
```

```python
import functools

import jax
import jax.numpy as jnp
from jax import lax
from jax.experimental import pallas as pl
from jax.experimental.pallas import tpu as pltpu
from jax.sharding import Mesh, PartitionSpec as P

ADAM_STEP = 100


beta_one = 0.9
beta_two = 0.95
step_size = 0.02
epsilon = 1e-08

Y = ("yh", "yl")
SIZES = {Y: 4, "z": 8, "x": 4, "c": 2}
f32, bf16 = jnp.float32, jnp.bfloat16


def shift(block, axis, by):
    size = SIZES[axis]
    return lax.ppermute(block, axis, [(i, (i + by) % size) for i in range(size)])


def both_ways(up, down, axis):
    return shift(up, axis, 1), shift(down, axis, -1)


def relay(below, above, axis):
    half = below.shape[0] // 2
    return both_ways(below[:half], above[half:], axis)


def order_four(axis):
    me = lax.axis_index(axis)
    return [me, (me + 3) % 4, (me + 1) % 4, (me + 2) % 4]


def facing(block):
    return lax.ppermute(block, Y, [(i, 3 - i) for i in range(4)])


def beside(block):
    return lax.ppermute(block, Y, [(i, i ^ 1) for i in range(4)])


def pick(part, at):
    return lax.dynamic_index_in_dim(part, at, 0, keepdims=False)


together = lax.optimization_barrier


def prepare_kernel(blocks_ref, places_ref, *refs):
    pieces, (projector_ref, whole_ref, low_ref, sum_ref) = refs[:-4], refs[-4:]
    step = pl.program_id(0)
    depth = pieces[0].shape[1]
    lanes = 128
    count = depth // lanes

    def put(piece, at):
        for i in range(count):
            start = pl.multiple_of(places_ref[at * count + i] * lanes, lanes)
            whole_ref[:, pl.ds(start, lanes)] = piece[:, i * lanes : (i + 1) * lanes]

    def add(piece, at):
        start = pl.multiple_of(blocks_ref[at] * depth, depth)
        return jnp.dot(
            piece[...], projector_ref[pl.ds(start, depth), :], preferred_element_type=f32
        )

    for side, (own, below, above, low, high) in enumerate((pieces[:5], pieces[5:])):
        for i, piece in enumerate((own, below, above)):
            put(piece, 4 * side + i)
        pl.when(step == 0)(functools.partial(put, low, 4 * side + 3))
        pl.when(step == 1)(functools.partial(put, high, 4 * side + 3))

    @pl.when(step == 0)
    def _():
        sum_ref[...] = add(pieces[0], 0)
        for at, piece in ((1, 1), (2, 2), (3, 3), (4, 5), (5, 6), (6, 7)):
            sum_ref[...] += add(pieces[piece], at)
        low_ref[...] = (sum_ref[...] + add(pieces[8], 7)).astype(bf16)


def prepare(mine, other, projector, blocks, places):
    rows, depth = mine[0].shape[0] // 2, mine[0].shape[1]
    features, rank = projector.shape
    moving = pl.BlockSpec((rows, depth), lambda i, *_: (i, 0))
    fixed = pl.BlockSpec((rows, depth), lambda i, *_: (0, 0))
    return pl.pallas_call(
        prepare_kernel,
        out_shape=(
            jax.ShapeDtypeStruct((2 * rows, features), bf16),
            jax.ShapeDtypeStruct((rows, rank), bf16),
        ),
        grid_spec=pltpu.PrefetchScalarGridSpec(
            num_scalar_prefetch=2,
            grid=(2,),
            in_specs=[moving, moving, moving, fixed, fixed] * 2
            + [pl.BlockSpec((features, rank), lambda i, *_: (0, 0))],
            out_specs=(
                pl.BlockSpec((rows, features), lambda i, *_: (i, 0)),
                pl.BlockSpec((rows, rank), lambda i, *_: (0, 0)),
            ),
            scratch_shapes=[pltpu.VMEM((rows, rank), f32)],
        ),
        compiler_params=pltpu.CompilerParams(vmem_limit_bytes=48 << 20),
        cost_estimate=pl.CostEstimate(
            flops=2 * rows * features * rank,
            bytes_accessed=2 * features * (4 * rows + rank),
            transcendentals=0,
        ),
    )(blocks, places, *mine, *other, projector)


def product_kernel(features, part_ref, left_ref, one, two, three, four, out_ref, whole_ref, sum_ref):
    half, lanes = one.shape[-2:]
    for i, (first, second) in enumerate(((one, two), (three, four))):
        columns = pl.ds(i * lanes, lanes)
        whole_ref[:, :half, columns] = first[...].reshape(-1, half, lanes)
        whole_ref[:, half:, columns] = second[...].reshape(-1, half, lanes)
    whole = whole_ref[...].reshape(-1, 2 * lanes)
    value = jnp.dot(left_ref[...], whole, preferred_element_type=f32)

    if whole.shape[0] == features:
        out_ref[...] = value.astype(out_ref.dtype)
        return

    @pl.when(pl.program_id(1) == 0)
    def _():
        sum_ref[...] = value

    @pl.when(pl.program_id(1) == 1)
    def _():
        out_ref[...] = (sum_ref[...] + value).astype(out_ref.dtype)


def product(left, part, weight, first, tiles, dtype, beside=None):
    rows, features = left.shape[0] // 2, left.shape[1]
    places, blocks, half, lanes = weight.shape
    pairs = blocks // 2 + 1

    halves = 2 if tiles == 1 else 1

    def block(at):
        return pl.BlockSpec(
            (places // halves, 1, half, lanes), lambda j, k, part: (k, at + 2 * j, 0, 0)
        )

    specs = [block(first), block(first + pairs), block(first + 1), block(first + 1 + pairs)]
    arrays = [weight] * 4
    if beside is not None:
        specs[3] = pl.BlockSpec((places // halves, half, lanes), lambda j, k, part: (k, 0, 0))
        arrays[3] = beside
    columns = tiles * 2 * lanes
    return pl.pallas_call(
        functools.partial(product_kernel, features),
        out_shape=jax.ShapeDtypeStruct((rows, columns), dtype),
        grid_spec=pltpu.PrefetchScalarGridSpec(
            num_scalar_prefetch=1,
            grid=(tiles, halves),
            in_specs=[
                pl.BlockSpec((rows, features // halves), lambda j, k, part: (part[0], k)),
                *specs,
            ],
            out_specs=pl.BlockSpec((rows, 2 * lanes), lambda j, k, part: (0, j)),
            scratch_shapes=[
                pltpu.VMEM((places // halves, 2 * half, 2 * lanes), bf16),
                pltpu.VMEM((rows, 2 * lanes), f32),
            ],
        ),
        compiler_params=pltpu.CompilerParams(vmem_limit_bytes=48 << 20),
        cost_estimate=pl.CostEstimate(
            flops=2 * rows * features * columns,
            bytes_accessed=2 * features * (rows + columns) + 4 * rows * columns,
            transcendentals=0,
        ),
    )(part, left, *arrays)


def changed(value, low_ref, pieces, columns):
    normed = jnp.concatenate([piece[:, columns] for piece in pieces], 0)
    change = jnp.dot(low_ref[...], normed, preferred_element_type=f32)
    return (value.astype(f32) - step_size * change).astype(bf16)


def most_kernel(group_ref, own_one, own_two, sent_one, low_ref, *refs):
    pieces, out_ref = refs[:-1], refs[-1]
    cut = own_one.shape[1]
    first, second = slice(0, cut), slice(cut, out_ref.shape[1])

    @pl.when(pl.program_id(0) == 0)
    def _():
        out_ref[:, first] = changed(own_one[...], low_ref, pieces, first)
        out_ref[:, second] = changed(own_two[...], low_ref, pieces, second)

    @pl.when(pl.program_id(0) == 1)
    def _():
        out_ref[:, first] = changed(sent_one[...], low_ref, pieces, first)


def rest_kernel(group_ref, sent_ref, low_ref, *refs):
    pieces, out_ref = refs[:-2], refs[-1]
    out_ref[...] = changed(sent_ref[...], low_ref, pieces, slice(None))


def last(own, sent, low, normed, group):
    rows, rank = low.shape
    cut, rest = own[0].shape[1], own[1].shape[1]
    columns = cut + rest
    place = lambda j, group: (0, (j + group[0]) % 2)
    fixed = lambda j, group: (0, 0)
    group = group.reshape(1)

    def call(kernel, grid, in_specs, out_spec, width, aliases, *arrays):
        return pl.pallas_call(
            kernel,
            out_shape=jax.ShapeDtypeStruct((rows, 2 * columns), bf16),
            grid_spec=pltpu.PrefetchScalarGridSpec(
                num_scalar_prefetch=1, grid=grid, in_specs=in_specs, out_specs=out_spec
            ),
            input_output_aliases=aliases,
            compiler_params=pltpu.CompilerParams(vmem_limit_bytes=32 << 20),
            cost_estimate=pl.CostEstimate(
                flops=2 * rows * rank * width,
                bytes_accessed=5 * rows * width + 2 * rank * width,
                transcendentals=0,
            ),
        )(group, *arrays)

    most = call(
        most_kernel,
        (2,),
        [
            *[pl.BlockSpec(array.shape, fixed) for array in (*own, sent[0], low)],
            *[pl.BlockSpec((piece.shape[0], columns), place) for piece in normed],
        ],
        pl.BlockSpec((rows, columns), place),
        columns + cut,
        {},
        *own,
        sent[0],
        low,
        *normed,
    )
    at = lambda j, group: (0, (1 - group[0]) * (columns // rest) + cut // rest)
    return call(
        rest_kernel,
        (1,),
        [
            pl.BlockSpec(sent[1].shape, fixed),
            pl.BlockSpec(low.shape, fixed),
            *[pl.BlockSpec((piece.shape[0], rest), at) for piece in normed],
            pl.BlockSpec(memory_space=pl.ANY),
        ],
        pl.BlockSpec((rows, rest), at),
        rest,
        {3 + len(normed): 0},
        sent[1],
        low,
        *normed,
        most,
    )


def body(tokens, grad_out, projector, moment_one, moment_two, weight, next_tokens):
    width = tokens.shape[1]
    columns = weight.shape[1]
    core = lax.axis_index("c")
    x_places, y_places = order_four("x"), order_four(Y)

    def proj_of(x, c):
        return lax.dynamic_slice_in_dim(projector, (2 * x + c) * width, width, 0)

    def part_of(x, block):
        return jnp.dot(block, proj_of(x, core), preferred_element_type=f32)

    y = lax.axis_index(Y)
    side, group = columns // 2, y // 2
    lanes = 128
    count = side // lanes
    blocks = jnp.swapaxes(weight.reshape(-1, 2 * count, lanes), 0, 1)
    weight_own = lax.dynamic_slice_in_dim(blocks, group * count, count, 0)
    weight_facing = facing(lax.dynamic_slice_in_dim(blocks, (1 - group) * count, count, 0))
    below, above = both_ways(tokens, tokens, "x")
    partial = part_of(x_places[0], tokens)
    below, above, partial, weight_facing = together((below, above, partial, weight_facing))

    weight_pair = jnp.concatenate([weight_own, weight_facing], 1)
    weight_beside = beside(weight_pair[:-1])
    low, high = relay(below, above, "x")
    facing_next = facing(next_tokens)
    partial = partial + part_of(x_places[1], below) + part_of(x_places[2], above)
    low, high, partial, facing_next, weight_beside = together(
        (low, high, partial, facing_next, weight_beside)
    )

    gathered = lax.all_gather(jnp.concatenate([weight_pair, weight_beside], 0), "z", axis=0)
    partial = partial + part_of(x_places[3], jnp.concatenate([low, high], 0))
    reduced = (partial + shift(partial, "c", 1)).astype(bf16)
    part = lax.dot_general(
        reduced, grad_out, (((0,), (0,)), ((), ())), preferred_element_type=f32
    ).astype(bf16)
    pair_next = jnp.concatenate([next_tokens, facing_next], 0)
    (part,) = together((part,))

    part = part.reshape(4, -1, columns)
    half = part.shape[1] // 2
    distant = pick(part, y_places[3])
    low, high = both_ways(distant[:half], distant[half:], Y)
    next_below, next_above = both_ways(pair_next, pair_next, "x")
    low, high = together((low, high))

    up, down = pick(part, y_places[2]).astype(f32), pick(part, y_places[1]).astype(f32)
    up = jnp.concatenate([up[:half] + low.astype(f32), up[half:]], 0).astype(bf16)
    down = jnp.concatenate([down[:half], down[half:] + high.astype(f32)], 0).astype(bf16)
    below, above = both_ways(up, down, Y)
    summed = pick(part, y_places[0]).astype(f32) + below.astype(f32) + above.astype(f32)
    (summed,) = together((summed.astype(bf16).reshape(8, -1, columns),))

    low_grad = lax.all_to_all(summed, "z", 0, 0)
    next_low, next_high = relay(next_below, next_above, "x")
    low_grad, next_low, next_high = together((low_grad, next_low, next_high))

    low_grad = jnp.sum(low_grad.astype(f32), 0)
    new_first = beta_one * moment_one + (1.0 - beta_one) * low_grad
    new_second = beta_two * moment_two + (1.0 - beta_two) * low_grad * low_grad
    first_fix = 1.0 - beta_one**ADAM_STEP
    second_fix = 1.0 - beta_two**ADAM_STEP
    normed = (new_first / first_fix / (jnp.sqrt(new_second / second_fix) + epsilon)).astype(bf16)
    normed = lax.all_to_all(jnp.broadcast_to(normed[None], (8, *normed.shape)), "z", 0, 0)
    normed = normed.reshape(-1, columns)
    mine = [pair_next, next_below, next_above, next_low, next_high]
    other = [shift(piece, "c", 1) for piece in mine]
    blocks = [(x, c) for c in (core, 1 - core) for x in x_places]
    natural = jnp.stack([2 * x + c for x, c in blocks])
    gathered_at = []
    for x, c in blocks:
        place = jnp.where(x == y, 0, jnp.where(x == 3 - y, 1, jnp.where(x == y ^ 1, 2, 3)))
        gathered_at += [4 * (4 * c + i) + place for i in range(4)]
    full_next, low_next = prepare(mine, other, projector, natural, jnp.stack(gathered_at))
    size = low_next.shape[1] // 4
    low_next = jnp.concatenate(
        [lax.dynamic_slice_in_dim(low_next, place * size, size, 1) for place in (y, y ^ 1, 3 - y, 3 - (y ^ 1))],
        1,
    )
    normed, full_next, low_next = together((normed, full_next, low_next))

    normed_beside, normed_facing = beside(normed), facing(normed)
    own_part, sent_part = jnp.zeros(1, jnp.int32), jnp.ones(1, jnp.int32)
    late = beside(gathered[:, count - 1])
    tiles = count // 2 - 1
    sent_one = product(full_next, sent_part, gathered, 0, tiles, bf16)
    normed_beside, normed_facing, sent_one, full_next = together(
        (normed_beside, normed_facing, sent_one, full_next)
    )

    sent_one = facing(sent_one)
    normed_far = beside(normed_facing)
    own_one = product(full_next, own_part, gathered, 0, tiles, f32)
    late, own_one, full_next = together((late, own_one, full_next))

    sent_two = product(full_next, sent_part, gathered, count - 2, 1, bf16, late)
    sent_two, full_next = together((sent_two, full_next))

    sent_two = facing(sent_two)
    own_two = product(full_next, own_part, gathered, count - 2, 1, f32, late)
    pieces = (normed, normed_beside, normed_facing, normed_far)
    gate = last((own_one, own_two), (sent_one, sent_two), low_next, pieces, group)
    return (gate, new_first, new_second)


def solution(mesh):
    split = Mesh(mesh.devices.reshape(2, 2, 8, 4, 2), (*Y, "z", "x", "c"))
    both = P((*Y, "z"), ("x", "c"))
    return jax.shard_map(
        body,
        mesh=split,
        in_specs=(both, both, P(), both, both, both, both),
        out_specs=(both, both, both),
        check_vma=False,
    )
```

```python
import functools

import jax
import jax.numpy as jnp
from jax import lax
from jax.experimental import pallas as pl
from jax.experimental.pallas import tpu as pltpu
from jax.sharding import Mesh, PartitionSpec as P

ADAM_STEP = 100


beta_one = 0.9
beta_two = 0.95
step_size = 0.02
epsilon = 1e-08

Y = ("yh", "yl")
SIZES = {Y: 4, "z": 8, "x": 4, "c": 2}
f32, bf16 = jnp.float32, jnp.bfloat16


def shift(block, axis, by):
    size = SIZES[axis]
    return lax.ppermute(block, axis, [(i, (i + by) % size) for i in range(size)])


def both_ways(up, down, axis):
    return shift(up, axis, 1), shift(down, axis, -1)


def relay(below, above, axis):
    half = below.shape[0] // 2
    return both_ways(below[:half], above[half:], axis)


def order_four(axis):
    me = lax.axis_index(axis)
    return [me, (me + 3) % 4, (me + 1) % 4, (me + 2) % 4]


def facing(block):
    return lax.ppermute(block, Y, [(i, 3 - i) for i in range(4)])


def beside(block):
    return lax.ppermute(block, Y, [(i, i ^ 1) for i in range(4)])


def pick(part, at):
    return lax.dynamic_index_in_dim(part, at, 0, keepdims=False)


together = lax.optimization_barrier


def prepare_kernel(blocks_ref, places_ref, *refs):
    pieces, (projector_ref, whole_ref, low_ref, sum_ref) = refs[:-4], refs[-4:]
    step = pl.program_id(0)
    depth = pieces[0].shape[1]
    lanes = 128
    count = depth // lanes

    def put(piece, at):
        for i in range(count):
            start = pl.multiple_of(places_ref[at * count + i] * lanes, lanes)
            whole_ref[:, pl.ds(start, lanes)] = piece[:, i * lanes : (i + 1) * lanes]

    def add(piece, at):
        start = pl.multiple_of(blocks_ref[at] * depth, depth)
        return jnp.dot(
            piece[...], projector_ref[pl.ds(start, depth), :], preferred_element_type=f32
        )

    for side, (own, below, above, low, high) in enumerate((pieces[:5], pieces[5:])):
        for i, piece in enumerate((own, below, above)):
            put(piece, 4 * side + i)
        pl.when(step == 0)(functools.partial(put, low, 4 * side + 3))
        pl.when(step == 1)(functools.partial(put, high, 4 * side + 3))

    @pl.when(step == 0)
    def _():
        sum_ref[...] = add(pieces[0], 0)
        for at, piece in ((1, 1), (2, 2), (3, 3), (4, 5), (5, 6), (6, 7)):
            sum_ref[...] += add(pieces[piece], at)
        low_ref[...] = (sum_ref[...] + add(pieces[8], 7)).astype(bf16)


def prepare(mine, other, projector, blocks, places):
    rows, depth = mine[0].shape[0] // 2, mine[0].shape[1]
    features, rank = projector.shape
    moving = pl.BlockSpec((rows, depth), lambda i, *_: (i, 0))
    fixed = pl.BlockSpec((rows, depth), lambda i, *_: (0, 0))
    return pl.pallas_call(
        prepare_kernel,
        out_shape=(
            jax.ShapeDtypeStruct((2 * rows, features), bf16),
            jax.ShapeDtypeStruct((rows, rank), bf16),
        ),
        grid_spec=pltpu.PrefetchScalarGridSpec(
            num_scalar_prefetch=2,
            grid=(2,),
            in_specs=[moving, moving, moving, fixed, fixed] * 2
            + [pl.BlockSpec((features, rank), lambda i, *_: (0, 0))],
            out_specs=(
                pl.BlockSpec((rows, features), lambda i, *_: (i, 0)),
                pl.BlockSpec((rows, rank), lambda i, *_: (0, 0)),
            ),
            scratch_shapes=[pltpu.VMEM((rows, rank), f32)],
        ),
        compiler_params=pltpu.CompilerParams(vmem_limit_bytes=48 << 20),
        cost_estimate=pl.CostEstimate(
            flops=2 * rows * features * rank,
            bytes_accessed=2 * features * (4 * rows + rank),
            transcendentals=0,
        ),
    )(blocks, places, *mine, *other, projector)


def product_kernel(part_ref, left_ref, *refs):
    blocks, (out_ref, whole_ref, sum_ref) = refs[:-3], refs[-3:]
    half, lanes = blocks[0].shape[-2:]
    for i in range(len(blocks) // 2):
        columns = pl.ds(i * lanes, lanes)
        whole_ref[:, :half, columns] = blocks[2 * i][...].reshape(-1, half, lanes)
        whole_ref[:, half:, columns] = blocks[2 * i + 1][...].reshape(-1, half, lanes)
    whole = whole_ref[...].reshape(-1, whole_ref.shape[2])
    value = jnp.dot(left_ref[...], whole, preferred_element_type=f32)

    @pl.when(pl.program_id(0) == 0)
    def _():
        sum_ref[...] = value

    @pl.when(pl.program_id(0) == 1)
    def _():
        out_ref[...] = (sum_ref[...] + value).astype(out_ref.dtype)


def product(left, part, weight, first, tiles, dtype, beside=None):
    rows, features = left.shape[0] // 2, left.shape[1]
    places, blocks, half, lanes = weight.shape
    pairs = blocks // 2 + 1
    specs = [
        pl.BlockSpec((places // 2, 1, half, lanes), lambda k, part, at=at: (k, at, 0, 0))
        for i in range(2 * tiles)
        for at in (first + i, min(first + i + pairs, blocks - 1))
    ]
    arrays = [weight] * len(specs)
    if beside is not None:
        specs[-1] = pl.BlockSpec((places // 2, half, lanes), lambda k, part: (k, 0, 0))
        arrays[-1] = beside
    columns = tiles * 2 * lanes
    return pl.pallas_call(
        product_kernel,
        out_shape=jax.ShapeDtypeStruct((rows, columns), dtype),
        grid_spec=pltpu.PrefetchScalarGridSpec(
            num_scalar_prefetch=1,
            grid=(2,),
            in_specs=[
                pl.BlockSpec((rows, features // 2), lambda k, part: (part[0], k)),
                *specs,
            ],
            out_specs=pl.BlockSpec((rows, columns), lambda k, part: (0, 0)),
            scratch_shapes=[
                pltpu.VMEM((places // 2, 2 * half, columns), bf16),
                pltpu.VMEM((rows, columns), f32),
            ],
        ),
        compiler_params=pltpu.CompilerParams(vmem_limit_bytes=48 << 20),
        cost_estimate=pl.CostEstimate(
            flops=2 * rows * features * columns,
            bytes_accessed=2 * features * (rows + columns) + 4 * rows * columns,
            transcendentals=0,
        ),
    )(part, left, *arrays)


def changed(value, low_ref, pieces, columns):
    normed = jnp.concatenate([piece[:, columns] for piece in pieces], 0)
    change = jnp.dot(low_ref[...], normed, preferred_element_type=f32)
    return (value.astype(f32) - step_size * change).astype(bf16)


def most_kernel(group_ref, own_one, own_two, sent_one, low_ref, *refs):
    pieces, out_ref = refs[:-1], refs[-1]
    cut = own_one.shape[1]
    first, second = slice(0, cut), slice(cut, out_ref.shape[1])

    @pl.when(pl.program_id(0) == 0)
    def _():
        out_ref[:, first] = changed(own_one[...], low_ref, pieces, first)
        out_ref[:, second] = changed(own_two[...], low_ref, pieces, second)

    @pl.when(pl.program_id(0) == 1)
    def _():
        out_ref[:, first] = changed(sent_one[...], low_ref, pieces, first)


def rest_kernel(group_ref, sent_ref, low_ref, *refs):
    pieces, out_ref = refs[:-2], refs[-1]
    out_ref[...] = changed(sent_ref[...], low_ref, pieces, slice(None))


def last(own, sent, low, normed, group):
    rows, rank = low.shape
    cut, rest = own[0].shape[1], own[1].shape[1]
    columns = cut + rest
    place = lambda j, group: (0, (j + group[0]) % 2)
    fixed = lambda j, group: (0, 0)
    group = group.reshape(1)

    def call(kernel, grid, in_specs, out_spec, width, aliases, *arrays):
        return pl.pallas_call(
            kernel,
            out_shape=jax.ShapeDtypeStruct((rows, 2 * columns), bf16),
            grid_spec=pltpu.PrefetchScalarGridSpec(
                num_scalar_prefetch=1, grid=grid, in_specs=in_specs, out_specs=out_spec
            ),
            input_output_aliases=aliases,
            compiler_params=pltpu.CompilerParams(vmem_limit_bytes=32 << 20),
            cost_estimate=pl.CostEstimate(
                flops=2 * rows * rank * width,
                bytes_accessed=5 * rows * width + 2 * rank * width,
                transcendentals=0,
            ),
        )(group, *arrays)

    most = call(
        most_kernel,
        (2,),
        [
            *[pl.BlockSpec(array.shape, fixed) for array in (*own, sent[0], low)],
            *[pl.BlockSpec((piece.shape[0], columns), place) for piece in normed],
        ],
        pl.BlockSpec((rows, columns), place),
        columns + cut,
        {},
        *own,
        sent[0],
        low,
        *normed,
    )
    at = lambda j, group: (0, (1 - group[0]) * (columns // rest) + cut // rest)
    return call(
        rest_kernel,
        (1,),
        [
            pl.BlockSpec(sent[1].shape, fixed),
            pl.BlockSpec(low.shape, fixed),
            *[pl.BlockSpec((piece.shape[0], rest), at) for piece in normed],
            pl.BlockSpec(memory_space=pl.ANY),
        ],
        pl.BlockSpec((rows, rest), at),
        rest,
        {3 + len(normed): 0},
        sent[1],
        low,
        *normed,
        most,
    )


def body(tokens, grad_out, projector, moment_one, moment_two, weight, next_tokens):
    width = tokens.shape[1]
    columns = weight.shape[1]
    core = lax.axis_index("c")
    x_places, y_places = order_four("x"), order_four(Y)

    def proj_of(x, c):
        return lax.dynamic_slice_in_dim(projector, (2 * x + c) * width, width, 0)

    def part_of(x, block):
        return jnp.dot(block, proj_of(x, core), preferred_element_type=f32)

    y = lax.axis_index(Y)
    side, group = columns // 2, y // 2
    lanes = 128
    count = side // lanes
    blocks = jnp.swapaxes(weight.reshape(-1, 2 * count, lanes), 0, 1)
    weight_own = lax.dynamic_slice_in_dim(blocks, group * count, count, 0)
    weight_facing = facing(lax.dynamic_slice_in_dim(blocks, (1 - group) * count, count, 0))
    below, above = both_ways(tokens, tokens, "x")
    partial = part_of(x_places[0], tokens)
    below, above, partial, weight_facing = together((below, above, partial, weight_facing))

    weight_pair = jnp.concatenate([weight_own, weight_facing], 1)
    weight_beside = beside(weight_pair[:-1])
    low, high = relay(below, above, "x")
    facing_next = facing(next_tokens)
    partial = partial + part_of(x_places[1], below) + part_of(x_places[2], above)
    low, high, partial, facing_next, weight_beside = together(
        (low, high, partial, facing_next, weight_beside)
    )

    gathered = lax.all_gather(jnp.concatenate([weight_pair, weight_beside], 0), "z", axis=0)
    partial = partial + part_of(x_places[3], jnp.concatenate([low, high], 0))
    reduced = (partial + shift(partial, "c", 1)).astype(bf16)
    part = lax.dot_general(
        reduced, grad_out, (((0,), (0,)), ((), ())), preferred_element_type=f32
    ).astype(bf16)
    pair_next = jnp.concatenate([next_tokens, facing_next], 0)
    (part,) = together((part,))

    part = part.reshape(4, -1, columns)
    half = part.shape[1] // 2
    distant = pick(part, y_places[3])
    low, high = both_ways(distant[:half], distant[half:], Y)
    next_below, next_above = both_ways(pair_next, pair_next, "x")
    low, high = together((low, high))

    up, down = pick(part, y_places[2]).astype(f32), pick(part, y_places[1]).astype(f32)
    up = jnp.concatenate([up[:half] + low.astype(f32), up[half:]], 0).astype(bf16)
    down = jnp.concatenate([down[:half], down[half:] + high.astype(f32)], 0).astype(bf16)
    below, above = both_ways(up, down, Y)
    summed = pick(part, y_places[0]).astype(f32) + below.astype(f32) + above.astype(f32)
    (summed,) = together((summed.astype(bf16).reshape(8, -1, columns),))

    low_grad = lax.all_to_all(summed, "z", 0, 0)
    next_low, next_high = relay(next_below, next_above, "x")
    low_grad, next_low, next_high = together((low_grad, next_low, next_high))

    low_grad = jnp.sum(low_grad.astype(f32), 0)
    new_first = beta_one * moment_one + (1.0 - beta_one) * low_grad
    new_second = beta_two * moment_two + (1.0 - beta_two) * low_grad * low_grad
    first_fix = 1.0 - beta_one**ADAM_STEP
    second_fix = 1.0 - beta_two**ADAM_STEP
    normed = (new_first / first_fix / (jnp.sqrt(new_second / second_fix) + epsilon)).astype(bf16)
    normed = lax.all_to_all(jnp.broadcast_to(normed[None], (8, *normed.shape)), "z", 0, 0)
    normed = normed.reshape(-1, columns)
    mine = [pair_next, next_below, next_above, next_low, next_high]
    other = [shift(piece, "c", 1) for piece in mine]
    blocks = [(x, c) for c in (core, 1 - core) for x in x_places]
    natural = jnp.stack([2 * x + c for x, c in blocks])
    gathered_at = []
    for x, c in blocks:
        place = jnp.where(x == y, 0, jnp.where(x == 3 - y, 1, jnp.where(x == y ^ 1, 2, 3)))
        gathered_at += [4 * (4 * c + i) + place for i in range(4)]
    full_next, low_next = prepare(mine, other, projector, natural, jnp.stack(gathered_at))
    size = low_next.shape[1] // 4
    low_next = jnp.concatenate(
        [lax.dynamic_slice_in_dim(low_next, place * size, size, 1) for place in (y, y ^ 1, 3 - y, 3 - (y ^ 1))],
        1,
    )
    normed, full_next, low_next = together((normed, full_next, low_next))

    normed_beside, normed_facing = beside(normed), facing(normed)
    own_part, sent_part = jnp.zeros(1, jnp.int32), jnp.ones(1, jnp.int32)
    late = beside(gathered[:, count - 1])
    tiles = count // 2 - 1
    sent_one = product(full_next, sent_part, gathered, 0, tiles, bf16)
    normed_beside, normed_facing, sent_one, full_next = together(
        (normed_beside, normed_facing, sent_one, full_next)
    )

    sent_one = facing(sent_one)
    normed_far = beside(normed_facing)
    own_one = product(full_next, own_part, gathered, 0, tiles, f32)
    late, own_one, full_next = together((late, own_one, full_next))

    sent_two = product(full_next, sent_part, gathered, count - 2, 1, bf16, late)
    sent_two, full_next = together((sent_two, full_next))

    sent_two = facing(sent_two)
    own_two = product(full_next, own_part, gathered, count - 2, 1, f32, late)
    pieces = (normed, normed_beside, normed_facing, normed_far)
    gate = last((own_one, own_two), (sent_one, sent_two), low_next, pieces, group)
    return (gate, new_first, new_second)


def solution(mesh):
    split = Mesh(mesh.devices.reshape(2, 2, 8, 4, 2), (*Y, "z", "x", "c"))
    both = P((*Y, "z"), ("x", "c"))
    return jax.shard_map(
        body,
        mesh=split,
        in_specs=(both, both, P(), both, both, both, both),
        out_specs=(both, both, both),
        check_vma=False,
    )
```
